32 devices in a mesh: view: 2 (over y), ty: 4 (over z), tx: 4 (over x, core).
Axes of the slice: x: 2, y: 2, z: 4, core: 2. Of those that a mesh axis runs over, the one named last changes fastest.
Arguments:
- views_data: float32 [2, 64, 128, 2048], P('view', None, 'ty', 'tx'), may hold values from 0.5 to 2
- psf_axial: float32 [2, 21], P('view'), may hold values from 0.2 to 1
- psf_rows: float32 [2, 7], P('view'), may hold values from 0.2 to 1
- psf_cols: float32 [2, 7], P('view'), may hold values from 0.2 to 1
Outputs:
- estimate: float32 [64, 128, 2048], P(None, 'ty', 'tx')
The draws below stay inside these ranges and needn't reach their ends.
All inputs are finite; a program needn't handle non-finite values.
Results may differ from the reference program's by a relative error of at most 0.0001.
Values sent between devices are 32-bit elements; how exact they have to be, the bound alone decides.
A program may use at most 128 MiB of HBM per device.

```python
import math
import jax
import jax.numpy as jnp
from jax import lax

PLANES = 64
KZ = 21
KL = 7
ITERS = 2
NY = 128
NX = 2048


def steps_of(stream_key, extent, shards, smallest, top_value):
    level = 1.0
    for axis_at, blocks in shards:
        steps = jax.random.uniform(jax.random.fold_in(jax.random.fold_in(stream_key, 6), axis_at), (blocks,), jnp.float32, smallest / len(shards), top_value / len(shards))
        level = level * jnp.repeat(jnp.exp(steps), extent[axis_at] // blocks).reshape((-1,) + (1,) * (len(extent) - 1 - axis_at))
    return level


def setup_inputs(seed: int = 0) -> dict:
    arg_keys = jax.random.split(jax.random.key(seed), 5)
    return {
        "views_data": jnp.clip(0.5 + 1.5 * jax.random.uniform(arg_keys[0], (2, PLANES, NY, NX), jnp.float32) ** steps_of(arg_keys[0], (2, PLANES, NY, NX), ((0, 2), (2, 4), (3, 4)), -0.2, 0.2), 0.5, 2.0),
        "psf_axial": jnp.clip(jnp.exp(math.log(1.0) - 1.609438 * jax.random.uniform(arg_keys[1], (2, KZ), jnp.float32) ** steps_of(arg_keys[1], (2, KZ), ((0, 2),), -0.2, 0.2)), 0.2, 1.0),
        "psf_rows": jnp.clip(jnp.exp(math.log(1.0) - 1.609438 * jax.random.uniform(arg_keys[2], (2, KL), jnp.float32) ** steps_of(arg_keys[2], (2, KL), ((0, 2),), -0.2, 0.2)), 0.2, 1.0),
        "psf_cols": jnp.clip(jnp.exp(math.log(1.0) - 1.609438 * jax.random.uniform(arg_keys[3], (2, KL), jnp.float32) ** steps_of(arg_keys[3], (2, KL), ((0, 2),), -0.2, 0.2)), 0.2, 1.0),
    }


def taps_pass(field, kernel, axis, length):
    running = kernel[0] * lax.slice_in_dim(field, 0, length, axis=axis)
    for offset in range(1, kernel.shape[0]):
        running = running + kernel[offset] * lax.slice_in_dim(field, offset, offset + length, axis=axis)
    return running


def padded_pass(field, kernel, axis):
    half_width = kernel.shape[0] // 2
    widths = [(0, 0), (0, 0), (0, 0)]
    widths[axis] = (half_width, half_width)
    return taps_pass(jnp.pad(field, widths), kernel, axis, field.shape[axis])


def blur_forward(field, kernel_z, kernel_y, kernel_x):
    field = padded_pass(field, kernel_z, 0)
    field = padded_pass(field, kernel_y, 1)
    return padded_pass(field, kernel_x, 2)


def blur_adjoint(field, kernel_z, kernel_y, kernel_x):
    field = padded_pass(field, kernel_x[::-1], 2)
    field = padded_pass(field, kernel_y[::-1], 1)
    return padded_pass(field, kernel_z[::-1], 0)


def reference(views_data, psf_axial, psf_rows, psf_cols):
    estimate = (views_data[0] + views_data[1]) * 0.5
    kernels = []
    for viewer in range(2):
        kernels.append((psf_axial[viewer] / jnp.sum(psf_axial[viewer]),
                        psf_rows[viewer] / jnp.sum(psf_rows[viewer]),
                        psf_cols[viewer] / jnp.sum(psf_cols[viewer])))
    for repeat in range(ITERS):
        factors = []
        for viewer in range(2):
            kernel_z, kernel_y, kernel_x = kernels[viewer]
            blurred = blur_forward(estimate, kernel_z, kernel_y, kernel_x)
            ratio = views_data[viewer] / blurred
            factors.append(blur_adjoint(ratio, kernel_z, kernel_y, kernel_x))
        estimate = estimate * ((factors[0] + factors[1]) * 0.5)
    return estimate
```

```python
import functools

import jax
import jax.numpy as jnp
from jax import lax
from jax.experimental import pallas as pl
from jax.experimental.pallas import tpu as pltpu
from jax.sharding import PartitionSpec as P

LANES = 128
CHUNK = 4
F32 = jnp.float32
BF16 = jnp.bfloat16


def split(value):
    high = value.astype(BF16)
    low = (value - high.astype(F32)).astype(BF16)
    return high, low


def split_matrix(value):
    high = lax.reduce_precision(value, 8, 7)
    return high.astype(BF16), (value - high).astype(BF16)


def banded(taps, position, valid):
    radius = taps.shape[0] // 2
    offset = position[:, None] - position[None, :] + radius
    matrix = jnp.zeros(offset.shape, F32)
    for tap in range(taps.shape[0]):
        matrix = matrix + jnp.where(offset == tap, taps[tap], 0.0)
    return jnp.where(valid[:, None] & valid[None, :], matrix, 0.0)


def piece_kernel(
    first, start, count, margins, *refs
):
    ky_ref, main_a, main_b, strips, wz_ref, bx_ref = refs[:6]
    refs = refs[6:]
    if not first:
        r1_in, e1_in, r2_in = refs[:3]
        refs = refs[3:]
    out_ref, r1_out, e1_out, r2_out = refs[:4]
    rec, est0, r1, e1, r2, sems = refs[4:]

    radius = margins
    carry = 2 * radius
    planes = rec.shape[2]
    width = main_a.shape[2]
    n_rec = rec.shape[1]
    rec_at = start + 4 * radius - n_rec + count + 4 * radius
    n_est0 = est0.shape[0]
    copies = []
    for view, main in enumerate((main_a, main_b)):
        copies.append(pltpu.make_async_copy(
            main.at[pl.ds(rec_at, n_rec)], rec.at[view, :, :, pl.ds(0, width)], sems.at[view]))
        copies.append(pltpu.make_async_copy(
            strips.at[view, pl.ds(rec_at, n_rec)],
            rec.at[view, :, :, pl.ds(width, LANES)], sems.at[2 + view]))
    if not first:
        copies.append(pltpu.make_async_copy(r1_in, r1.at[:, pl.ds(0, carry)], sems.at[4]))
        copies.append(pltpu.make_async_copy(e1_in, e1.at[pl.ds(0, carry)], sems.at[5]))
        copies.append(pltpu.make_async_copy(r2_in, r2.at[:, pl.ds(0, carry)], sems.at[6]))
    for copy in copies:
        copy.start()
    for copy in copies:
        copy.wait()

    end0 = start + count + 8 * radius
    end1 = end0 - radius
    end2 = end1 - radius
    end3 = end2 - radius
    end4 = end3 - radius
    at_rec = end0 - n_rec
    at0 = end0 - n_est0
    at1 = end1 - r1.shape[1]
    at2 = end2 - e1.shape[0]
    at3 = end3 - r2.shape[1]

    def average(row, _):
        source = at0 - at_rec + row
        est0[row] = (rec[0, source] + rec[1, source]) * 0.5
        return 0

    lax.fori_loop(0, n_est0, average, 0)

    def spread(load, taps, view, direction, size):
        parts = []
        for row in range(size):
            total = taps(0) * load(row)
            for tap in range(1, 2 * radius + 1):
                total = total + taps(tap) * load(row + tap)
            high, low = split(total)
            passed = jnp.dot(
                wz_ref[view, direction], jnp.concatenate([high, low, high], axis=0),
                preferred_element_type=F32)
            high, low = split(passed)
            parts.append(jnp.concatenate([high, low, high], axis=1))
        return jnp.dot(
            jnp.concatenate(parts, axis=0), bx_ref[view, direction], preferred_element_type=F32)

    def in_chunks(total, body):
        full = total // CHUNK

        def step(index, _):
            body(index * CHUNK, CHUNK)
            return 0

        if full:
            lax.fori_loop(0, full, step, 0)
        if total % CHUNK:
            body(full * CHUNK, total % CHUNK)

    def blur(source, source_at, target, target_at, skip):
        def body(begin, size):
            row0 = skip + begin
            for view in range(2):
                blurred = spread(
                    lambda j: source[target_at - radius - source_at + row0 + j],
                    lambda t: ky_ref[view, t], view, 0, size)
                blurred = blurred.reshape(size, planes, blurred.shape[1])
                recorded = rec[view, pl.ds(target_at - at_rec + row0, size)]
                target[view, pl.ds(row0, size)] = jnp.where(
                    recorded > 0, recorded / blurred, 0.0)
        in_chunks(target.shape[1] - skip, body)

    def adjoint(source, source_at, estimate, estimate_at, store, total, target_at, skip):
        def body(begin, size):
            row0 = skip + begin
            factor = 0.0
            for view in range(2):
                factor = factor + spread(
                    lambda j: source[view, target_at - radius - source_at + row0 + j],
                    lambda t: ky_ref[view, 2 * radius - t], view, 1, size)
            factor = factor.reshape(size, planes, factor.shape[1])
            old = estimate[pl.ds(target_at - estimate_at + row0, size)]
            store(row0, size, old * (factor * 0.5))
        in_chunks(total - skip, body)

    def store_e1(row0, size, value):
        e1[pl.ds(row0, size)] = value

    def store_out(row0, size, value):
        out_ref[pl.ds(row0, size)] = value[:, :, :width]

    skip = 0 if first else carry
    blur(est0, at0, r1, at1, skip)
    adjoint(r1, at1, est0, at0, store_e1, e1.shape[0], at2, skip)
    blur(e1, at2, r2, at3, skip)
    adjoint(r2, at3, e1, at2, store_out, count, end4 - count, 0)
    r1_out[...] = r1[:, pl.ds(r1.shape[1] - carry, carry)]
    e1_out[...] = e1[pl.ds(e1.shape[0] - carry, carry)]
    r2_out[...] = r2[:, pl.ds(r2.shape[1] - carry, carry)]


def piece(first, start, count, radius, ky, main_a, main_b, strips, wz, bx, state):
    planes, width = main_a.shape[1:]
    lanes = width + LANES
    carry = 2 * radius
    if first:
        n0, n1, n2, n3 = (count + 2 * radius * k for k in (4, 3, 2, 1))
        n_rec = n0
    else:
        n0 = n1 = n2 = n3 = count + carry
        n_rec = count + 3 * radius
    rows = count * 4 if not first else n1 + n2 + n3 + count
    any_space = pl.BlockSpec(memory_space=pl.ANY)
    vmem = pl.BlockSpec(memory_space=pltpu.VMEM)
    in_specs = [pl.BlockSpec(memory_space=pltpu.SMEM)] + [any_space] * 3 + [vmem] * 2
    in_specs += [] if first else [any_space] * 3
    out_shape = [
        jax.ShapeDtypeStruct((count, planes, width), F32),
        jax.ShapeDtypeStruct((2, carry, planes, lanes), F32),
        jax.ShapeDtypeStruct((carry, planes, lanes), F32),
        jax.ShapeDtypeStruct((2, carry, planes, lanes), F32),
    ]
    outs = pl.pallas_call(
        functools.partial(piece_kernel, first, start, count, radius),
        out_shape=out_shape,
        in_specs=in_specs,
        out_specs=[vmem] * 4,
        scratch_shapes=[
            pltpu.VMEM((2, n_rec, planes, lanes), F32),
            pltpu.VMEM((n0, planes, lanes), F32),
            pltpu.VMEM((2, n1, planes, lanes), F32),
            pltpu.VMEM((n2, planes, lanes), F32),
            pltpu.VMEM((2, n3, planes, lanes), F32),
            pltpu.SemaphoreType.DMA((7,)),
        ],
        cost_estimate=pl.CostEstimate(
            flops=rows * 2 * planes * lanes * 2 * (3 * lanes + 3 * planes + 60),
            bytes_accessed=n_rec * planes * lanes * 8, transcendentals=0),
        compiler_params=pltpu.CompilerParams(vmem_limit_bytes=50 * 2**20),
    )(ky, main_a, main_b, strips, wz, bx, *state)
    return outs[0], outs[1:]


def neighbours(low_edge, high_edge, axis):
    count = lax.axis_size(axis)
    forward = [(i, i + 1) for i in range(count - 1)]
    backward = [(i + 1, i) for i in range(count - 1)]
    return lax.ppermute(high_edge, axis, forward), lax.ppermute(low_edge, axis, backward)


def swap(value):
    return lax.ppermute(value, "view", [(0, 1), (1, 0)])


def per_device(views_data, psf_axial, psf_rows, psf_cols):
    recorded = views_data[0]
    planes, rows, cols = recorded.shape
    kz = psf_axial[0] / jnp.sum(psf_axial[0])
    ky = psf_rows[0] / jnp.sum(psf_rows[0])
    kx = psf_cols[0] / jnp.sum(psf_cols[0])
    radius = ky.shape[0] // 2
    reach = 4 * radius
    half = cols // 2
    mine = (lax.axis_index("view") + lax.axis_index("tx")) % 2

    main_a = lax.dynamic_slice_in_dim(recorded, mine * half, half, axis=2)
    main_b = swap(lax.dynamic_slice_in_dim(recorded, (1 - mine) * half, half, axis=2))

    edges = jnp.concatenate(
        [recorded[:, :, :reach], recorded[:, :, half - reach:half + reach],
         recorded[:, :, cols - reach:]], axis=2)
    edges = edges.transpose(2, 1, 0).reshape(4 * reach, rows * planes)
    before, after = neighbours(edges[:reach], edges[3 * reach:], "tx")
    sides = (jnp.concatenate([before, edges[2 * reach:3 * reach]]),
             jnp.concatenate([edges[reach:2 * reach], after]))
    strip_a = jnp.where(mine == 0, sides[0], sides[1])
    strip_b = swap(jnp.where(mine == 0, sides[1], sides[0]))
    strips = jnp.stack([strip_a, strip_b]).reshape(2, 2 * reach, rows, planes)
    above, below = neighbours(strips[:, :, :reach], strips[:, :, rows - reach:], "ty")
    strips = jnp.concatenate([above, strips, below], axis=2).transpose(0, 2, 3, 1)
    strips = jnp.pad(strips, ((0, 0), (0, 0), (0, 0), (0, LANES - 2 * reach)))

    def extend(main):
        above, below = neighbours(main[:, :reach], main[:, rows - reach:], "ty")
        return jnp.concatenate(
            [part.transpose(1, 0, 2) for part in (above, main, below)], axis=0)

    ext_a = extend(main_a)
    ext_b = extend(main_b)

    taps = jnp.concatenate([kz, ky, kx])
    taps_b = swap(taps)
    lane = jnp.arange(half + LANES)
    position = jnp.where(
        lane < half, lane,
        jnp.where(lane < half + reach, lane - half - reach, lane - reach))
    valid = lane < half + 2 * reach
    plane = jnp.arange(planes)
    always = plane >= 0
    kys, wz, bx = [], [], []
    n_z, n_y = kz.shape[0], ky.shape[0]
    for vector in (taps, taps_b):
        kz, ky, kx = vector[:n_z], vector[n_z:n_z + n_y], vector[n_z + n_y:]
        kys.append(ky)
        axial = banded(kz, plane, always)
        wz.append(jnp.stack([
            jnp.concatenate([high, high, low], axis=1)
            for high, low in (split_matrix(axial.T), split_matrix(axial))]))
        lateral = banded(kx, position, valid)
        bx.append(jnp.stack([
            jnp.concatenate([high, high, low], axis=0)
            for high, low in (split_matrix(lateral), split_matrix(lateral.T))]))
    kys, wz, bx = jnp.stack(kys), jnp.stack(wz), jnp.stack(bx)

    count = 8
    result = jnp.zeros((planes, rows, cols), F32)
    state = ()
    done = []
    for start in range(0, rows, count):
        own, state = piece(
            start == 0, start, count, radius, kys, ext_a, ext_b, strips, wz, bx, tuple(state))
        done.append((start, own, swap(own)))
    for start, own, other in done:
        result = lax.dynamic_update_slice(
            result, own.transpose(1, 0, 2), (0, start, mine * half))
        result = lax.dynamic_update_slice(
            result, other.transpose(1, 0, 2), (0, start, (1 - mine) * half))
    return result


def solution(mesh):
    placed = (P("view", None, "ty", "tx"), P("view", None), P("view", None), P("view", None))
    return jax.shard_map(
        per_device, mesh=mesh, in_specs=placed, out_specs=P(None, "ty", "tx"), check_vma=False
    )
```

```python
import functools

import jax
import jax.numpy as jnp
from jax import lax
from jax.experimental import pallas as pl
from jax.experimental.pallas import tpu as pltpu
from jax.sharding import PartitionSpec as P

LANES = 128
GROUP = 8
PACK = 4
F32 = jnp.float32
BF16 = jnp.bfloat16


def split(value):
    high = value.astype(BF16)
    low = (value - high.astype(F32)).astype(BF16)
    return high, low


def axial_matrix(taps_ref, view, direction, planes, count):
    radius = count // 2
    i = lax.broadcasted_iota(jnp.int32, (planes, planes), 0)
    j = lax.broadcasted_iota(jnp.int32, (planes, planes), 1)
    offset = (j - i if direction == 0 else i - j) + radius
    matrix = jnp.zeros((planes, planes), F32)
    for tap in range(count):
        matrix = jnp.where(offset == tap, taps_ref[view, tap], matrix)
    high, low = split(matrix)
    return jnp.concatenate([high, high, low], axis=1)


def piece_kernel(first, start, count, n_z, radius, rows, *refs):
    taps_ref = refs[0]
    segments = (refs[1:5], refs[5:9])
    strips = (refs[9:12], refs[12:15])
    refs = refs[15:]
    if not first:
        r1_in, e1_in, r2_in = refs[:3]
        refs = refs[3:]
    out_ref, r1_out, e1_out, r2_out = refs[:4]
    rec, est0, r1, e1, r2, wz, sems = refs[4:]

    reach = 4 * radius
    carry = 2 * radius
    taps = 2 * radius + 1
    planes = rec.shape[2]
    lanes = rec.shape[3]
    width = lanes - LANES
    n_rec = rec.shape[1]
    n_est0 = est0.shape[0]
    end0 = start + count + 2 * reach
    end1 = end0 - radius
    end2 = end1 - radius
    end3 = end2 - radius
    end4 = end3 - radius
    at_rec = end0 - n_rec
    at0 = end0 - n_est0
    at1 = end1 - r1.shape[1]
    at2 = end2 - e1.shape[0]
    at3 = end3 - r2.shape[1]

    copies = []
    for view in range(2):
        begin = 0
        for segment in segments[view]:
            size = segment.shape[0]
            low, high = max(begin, at_rec), min(begin + size, end0)
            if low < high:
                copies.append(pltpu.make_async_copy(
                    segment.at[pl.ds(low - begin, high - low)],
                    rec.at[view, pl.ds(low - at_rec, high - low), :, pl.ds(0, width)],
                    sems.at[len(copies)]))
            begin += size
    if not first:
        for source, target in (
            (r1_in, r1.at[:, pl.ds(0, carry)]),
            (e1_in, e1.at[pl.ds(0, carry)]),
            (r2_in, r2.at[:, pl.ds(0, carry)]),
        ):
            copies.append(pltpu.make_async_copy(source, target, sems.at[len(copies)]))
    for copy in copies:
        copy.start()

    for view in range(2):
        for direction in range(2):
            wz[view, direction] = axial_matrix(taps_ref, view, direction, planes, n_z)

    lane = lax.broadcasted_iota(jnp.int32, (planes, LANES), 1)
    beside = (lane < reach) | (lane >= LANES - reach)
    for view in range(2):
        above, mid, below = strips[view]
        for at in range(n_rec):
            row = at_rec + at - reach
            if row < 0:
                source, row = above, row + rows
            elif row >= rows:
                source, row = below, row - rows
            else:
                source = mid
            group, row = divmod(row, GROUP)
            value = source[row]
            if group:
                value = pltpu.roll(value, LANES - LANES // PACK * group, 1)
            rec[view, at, :, width:] = jnp.where(beside, value, 0.0)

    for copy in copies:
        copy.wait()

    def average(row, _):
        source = at0 - at_rec + row
        est0[row] = (rec[0, source] + rec[1, source]) * 0.5
        return 0

    lax.fori_loop(0, n_est0, average, 0)

    def spread(load, view, direction):
        def tap_of(base, tap):
            return taps_ref[view, base + (tap if direction == 0 else taps - 1 - tap)]

        total = tap_of(n_z, 0) * load(0)
        for tap in range(1, taps):
            total = total + tap_of(n_z, tap) * load(tap)
        high, low = split(total)
        passed = jnp.dot(
            wz[view, direction], jnp.concatenate([high, low, high], axis=0),
            preferred_element_type=F32)
        total = tap_of(n_z + taps, radius) * passed
        for tap in range(taps):
            if tap != radius:
                total = total + tap_of(n_z + taps, tap) * pltpu.roll(
                    passed, (radius - tap) % lanes, 1)
        return total

    def blur(source, source_at, target, target_at, skip):
        def body(index, _):
            row = skip + index
            for view in range(2):
                blurred = spread(
                    lambda j: source[target_at - radius - source_at + row + j], view, 0)
                recorded = rec[view, target_at - at_rec + row]
                target[view, row] = jnp.where(recorded > 0, recorded / blurred, 0.0)
            return 0
        lax.fori_loop(0, target.shape[1] - skip, body, 0)

    def adjoint(source, source_at, estimate, estimate_at, target, total, target_at, skip):
        def body(index, _):
            row = skip + index
            factors = [
                spread(
                    lambda j: source[view, target_at - radius - source_at + row + j], view, 1)
                for view in range(2)]
            old = estimate[target_at - estimate_at + row]
            value = old * ((factors[0] + factors[1]) * 0.5)
            target[row] = value[:, :target.shape[2]]
            return 0
        lax.fori_loop(0, total - skip, body, 0)

    skip = 0 if first else carry
    blur(est0, at0, r1, at1, skip)
    adjoint(r1, at1, est0, at0, e1, e1.shape[0], at2, skip)
    blur(e1, at2, r2, at3, skip)
    adjoint(r2, at3, e1, at2, out_ref, count, end4 - count, 0)
    r1_out[...] = r1[:, pl.ds(r1.shape[1] - carry, carry)]
    e1_out[...] = e1[pl.ds(e1.shape[0] - carry, carry)]
    r2_out[...] = r2[:, pl.ds(r2.shape[1] - carry, carry)]


def piece(first, start, count, n_z, radius, rows, taps, segments, strips, state):
    planes, width = segments[0].shape[1:]
    lanes = width + LANES
    carry = 2 * radius
    if first:
        n0, n1, n2, n3 = (count + 2 * radius * k for k in (4, 3, 2, 1))
        n_rec = n0
        work = n1 + n2 + n3 + count
    else:
        n0 = n1 = n2 = n3 = count + carry
        n_rec = count + 3 * radius
        work = 4 * count
    any_space = pl.BlockSpec(memory_space=pl.ANY)
    vmem = pl.BlockSpec(memory_space=pltpu.VMEM)
    in_specs = [pl.BlockSpec(memory_space=pltpu.SMEM)]
    in_specs += [any_space] * len(segments) + [vmem] * (len(strips) + len(state))
    out_shape = [
        jax.ShapeDtypeStruct((count, planes, width), F32),
        jax.ShapeDtypeStruct((2, carry, planes, lanes), F32),
        jax.ShapeDtypeStruct((carry, planes, lanes), F32),
        jax.ShapeDtypeStruct((2, carry, planes, lanes), F32),
    ]
    outs = pl.pallas_call(
        functools.partial(piece_kernel, first, start, count, n_z, radius, rows),
        out_shape=out_shape,
        in_specs=in_specs,
        out_specs=[vmem] * 4,
        scratch_shapes=[
            pltpu.VMEM((2, n_rec, planes, lanes), F32),
            pltpu.VMEM((n0, planes, lanes), F32),
            pltpu.VMEM((2, n1, planes, lanes), F32),
            pltpu.VMEM((n2, planes, lanes), F32),
            pltpu.VMEM((2, n3, planes, lanes), F32),
            pltpu.VMEM((2, 2, planes, 3 * planes), BF16),
            pltpu.SemaphoreType.DMA((11,)),
        ],
        cost_estimate=pl.CostEstimate(
            flops=work * 2 * planes * lanes * 6000,
            bytes_accessed=n_rec * planes * lanes * 8, transcendentals=0),
        compiler_params=pltpu.CompilerParams(vmem_limit_bytes=40 * 2**20),
    )(taps, *segments, *strips, *state)
    return outs[0], outs[1:]


def half_by_rows(recorded, which, begin, size):
    planes, _, cols = recorded.shape
    half = cols // 2

    def body(which_ref, in_ref, out_ref):
        out_ref[...] = jnp.swapaxes(in_ref[...], 0, 1)

    return pl.pallas_call(
        body,
        out_shape=jax.ShapeDtypeStruct((size, planes, half), F32),
        grid_spec=pltpu.PrefetchScalarGridSpec(
            num_scalar_prefetch=1,
            grid=(size // GROUP,),
            in_specs=[pl.BlockSpec(
                (planes, GROUP, half), lambda g, w: (0, begin // GROUP + g, w[0]))],
            out_specs=pl.BlockSpec((GROUP, planes, half), lambda g, w: (g, 0, 0)),
        ),
        cost_estimate=pl.CostEstimate(
            flops=0, bytes_accessed=size * planes * half * 8, transcendentals=0),
    )(which.reshape(1), recorded)


def packed_edges(low_rows, high_rows, reach):
    size, planes, half = low_rows.shape
    groups = size // GROUP

    def body(*refs):
        lane = lax.broadcasted_iota(jnp.int32, (GROUP, planes, LANES), 2)
        for side in range(2):
            keep = lane < reach if side == 0 else lane >= LANES - reach
            total = jnp.zeros((GROUP, planes, LANES), F32)
            for group in range(2 * groups):
                ref = refs[2 * side + group // groups]
                value = jnp.where(keep, ref[pl.ds(group % groups * GROUP, GROUP)], 0.0)
                if group:
                    value = pltpu.roll(value, LANES // PACK * group, 2)
                total = total + value
            refs[4 + side][...] = total

    first = pl.BlockSpec((size, planes, LANES), lambda g: (0, 0, 0))
    last = pl.BlockSpec((size, planes, LANES), lambda g: (0, 0, half // LANES - 1))
    edge = pl.BlockSpec((GROUP, planes, LANES), lambda g: (0, 0, 0))
    return pl.pallas_call(
        body,
        out_shape=[jax.ShapeDtypeStruct((GROUP, planes, LANES), F32)] * 2,
        grid=(1,),
        in_specs=[first, first, last, last],
        out_specs=[edge, edge],
    )(low_rows, high_rows, low_rows, high_rows)


def neighbours(low_edge, high_edge, axis):
    count = lax.axis_size(axis)
    forward = [(i, i + 1) for i in range(count - 1)]
    backward = [(i + 1, i) for i in range(count - 1)]
    return lax.ppermute(high_edge, axis, forward), lax.ppermute(low_edge, axis, backward)


def swap(value):
    return lax.ppermute(value, "view", [(0, 1), (1, 0)])


def per_device(views_data, psf_axial, psf_rows, psf_cols):
    recorded = views_data[0]
    planes, rows, cols = recorded.shape
    radius = psf_rows.shape[1] // 2
    reach = 4 * radius
    half = cols // 2
    mid = rows // 2
    mine = (lax.axis_index("view") + lax.axis_index("tx")) % 2

    sent_high = half_by_rows(recorded, 1 - mine, mid, mid)
    got_high = swap(sent_high)
    sent_low = half_by_rows(recorded, 1 - mine, 0, mid)
    got_low = swap(sent_low)
    own_high = half_by_rows(recorded, mine, mid, mid)
    own_low = half_by_rows(recorded, mine, 0, mid)

    own_taps = jnp.concatenate([
        psf_axial[0] / jnp.sum(psf_axial[0]), psf_rows[0] / jnp.sum(psf_rows[0]),
        psf_cols[0] / jnp.sum(psf_cols[0])])
    taps = jnp.stack([own_taps, swap(own_taps)])

    def extended(low, high):
        above, below = neighbours(low[:reach], high[mid - reach:], "ty")
        return above, low, high, below

    segments_own = extended(own_low, own_high)
    segments_got = extended(got_low, got_high)

    own_first, own_last = packed_edges(own_low, own_high, reach)
    sent_first, sent_last = packed_edges(sent_low, sent_high, reach)
    left = mine == 0
    before, after = neighbours(
        jnp.where(left, own_first, sent_first), jnp.where(left, sent_last, own_last), "tx")
    beside_left = before + jnp.where(left, sent_first, own_first)
    beside_right = jnp.where(left, own_last, sent_last) + after
    strip_own = jnp.where(left, beside_left, beside_right)
    strip_got = swap(jnp.where(left, beside_right, beside_left))
    strips = []
    for strip in (strip_own, strip_got):
        above, below = neighbours(strip, strip, "ty")
        strips += [above, strip, below]

    count = GROUP
    result = jnp.zeros((planes, rows, cols), F32)
    state = ()
    done = []
    for start in range(0, rows, count):
        segments, beside = [], []
        for view, parts in enumerate((segments_own, segments_got)):
            past = start + count + reach > rows
            segments += parts if past else parts[:3] + parts[:1]
            parts = strips[3 * view:3 * view + 3]
            beside += parts if past else parts[:2] + parts[:1]
        own, state = piece(
            start == 0, start, count, psf_axial.shape[1], radius, rows, taps,
            segments, beside, tuple(state))
        done.append((start, own, swap(own)))
    for start, own, other in done:
        result = lax.dynamic_update_slice(
            result, own.transpose(1, 0, 2), (0, start, mine * half))
        result = lax.dynamic_update_slice(
            result, other.transpose(1, 0, 2), (0, start, (1 - mine) * half))
    return result


def solution(mesh):
    placed = (P("view", None, "ty", "tx"), P("view", None), P("view", None), P("view", None))
    return jax.shard_map(
        per_device, mesh=mesh, in_specs=placed, out_specs=P(None, "ty", "tx"), check_vma=False
    )
```

```python
import functools

import jax
import jax.numpy as jnp
from jax import lax
from jax.experimental import pallas as pl
from jax.experimental.pallas import tpu as pltpu
from jax.sharding import PartitionSpec as P

LANES = 128
GROUP = 8
ROWS = 2
PART = 16
PACK = 4
F32 = jnp.float32
BF16 = jnp.bfloat16


def split(value):
    high = value.astype(BF16)
    low = (value - high.astype(F32)).astype(BF16)
    return high, low


def axial_matrix(taps_ref, view, direction, planes, count):
    radius = count // 2
    i = lax.broadcasted_iota(jnp.int32, (planes, planes), 0)
    j = lax.broadcasted_iota(jnp.int32, (planes, planes), 1)
    offset = (j - i if direction == 0 else i - j) + radius
    matrix = jnp.zeros((planes, planes), F32)
    for tap in range(count):
        matrix = jnp.where(offset == tap, taps_ref[view, tap], matrix)
    high, low = split(matrix)
    return jnp.concatenate([high, high, low], axis=1)


def slab_kernel(n_z, radius, rows, taps_ref, *refs):
    segments = (refs[0:4], refs[4:8])
    strips = (refs[8:11], refs[11:14])
    (out_ref, rec, est0, r1, e1, r2, stage, turned, wz,
     in_sems, own_sems, send_sems, recv_sems) = refs[14:]
    reach = 4 * radius
    taps = 2 * radius + 1
    n_rec, planes, lanes = rec.shape[1:]
    width = lanes - LANES
    groups = rows // GROUP
    view_at = lax.axis_index("view")
    mine = (view_at + lax.axis_index("tx")) % 2
    columns = pl.ds(pl.multiple_of(mine * width, LANES), width)

    barrier = pltpu.get_barrier_semaphore()
    pl.semaphore_signal(
        barrier, inc=1, device_id={"view": 1 - view_at}, device_id_type=pl.DeviceIdType.MESH)
    pl.semaphore_wait(barrier, 1)

    copies = []
    for view in range(2):
        begin = 0
        for segment in segments[view]:
            size = segment.shape[0]
            copies.append(pltpu.make_async_copy(
                segment, rec.at[view, pl.ds(begin, size), :, pl.ds(0, width)],
                in_sems.at[len(copies)]))
            begin += size
    for copy in copies:
        copy.start()

    for view in range(2):
        for direction in range(2):
            wz[view, direction] = axial_matrix(taps_ref, view, direction, planes, n_z)

    lane = lax.broadcasted_iota(jnp.int32, (planes, LANES), 1)
    beside = (lane < reach) | (lane >= LANES - reach)
    for view in range(2):
        above, mid, below = strips[view]
        for at in range(n_rec):
            row = at - reach
            if row < 0:
                source, row = above, row + rows
            elif row >= rows:
                source, row = below, row - rows
            else:
                source = mid
            group, row = divmod(row, GROUP)
            value = source[row]
            if group:
                value = pltpu.roll(value, LANES - LANES // PACK * group, 1)
            rec[view, at, :, width:] = jnp.where(beside, value, 0.0)

    for copy in copies:
        copy.wait()

    def tap_of(base, view, direction, tap):
        return taps_ref[view, base + (tap if direction == 0 else taps - 1 - tap)]

    def rows_and_planes(load, view, direction):
        highs, lows = [], []
        for part in range(0, planes, PART):
            total = tap_of(n_z, view, direction, 0) * load(0, part)
            for tap in range(1, taps):
                total = total + tap_of(n_z, view, direction, tap) * load(tap, part)
            high, low = split(total)
            highs.append(high)
            lows.append(low)
        return jnp.dot(
            wz[view, direction], jnp.concatenate(highs + lows + highs, axis=0),
            preferred_element_type=F32)

    def over_columns(field, view, direction):
        total = tap_of(n_z + taps, view, direction, radius) * field
        for tap in range(taps):
            if tap != radius:
                total = total + tap_of(n_z + taps, view, direction, tap) * pltpu.roll(
                    field, (radius - tap) % lanes, 1)
        return total

    def by_rows(begin, end, body):
        count = end - begin
        assert count % ROWS == 0

        def step(index, _):
            body([begin + index * ROWS + k for k in range(ROWS)])
            return 0
        lax.fori_loop(0, count // ROWS, step, 0)

    def blur(source, source_at, target, target_at, begin, end):
        def body(at):
            passed = [[rows_and_planes(
                lambda j, part: source[row - radius - source_at + j, pl.ds(part, PART)], view, 0)
                for view in range(2)] for row in at]
            for row, fields in zip(at, passed):
                for view in range(2):
                    for part in range(0, planes, PART):
                        blurred = over_columns(fields[view][part:part + PART], view, 0)
                        recorded = rec[view, row, pl.ds(part, PART)]
                        inverse = pl.reciprocal(blurred, approx=True)
                        inverse = inverse * (2.0 - blurred * inverse)
                        target[view, row - target_at, pl.ds(part, PART)] = jnp.where(
                            recorded > 0, recorded * inverse, 0.0)
        by_rows(begin, end, body)

    def adjoint(source, source_at, estimate, estimate_at, store, begin, end):
        def body(at):
            passed = [[rows_and_planes(
                lambda j, part: source[
                    view, row - radius - source_at + j, pl.ds(part, PART)], view, 1)
                for view in range(2)] for row in at]
            for row, fields in zip(at, passed):
                for part in range(0, planes, PART):
                    factor = (over_columns(fields[0][part:part + PART], 0, 1)
                              + over_columns(fields[1][part:part + PART], 1, 1))
                    old = estimate[row - estimate_at, pl.ds(part, PART)]
                    store(row, part, old * (factor * 0.5))
        by_rows(begin, end, body)

    def store_e1(row, part, value):
        e1[row - 2 * radius, pl.ds(part, PART)] = value

    sends = []
    for group in range(groups):
        ends = [(group + 1) * GROUP + reach + k * radius for k in (4, 3, 2, 1, 0)]
        begins = [0 if group == 0 else end - GROUP for end in ends]
        if group == 0:
            begins = [k * radius for k in range(5)]

        def average(row, _):
            est0[row] = (rec[0, row] + rec[1, row]) * 0.5
            return 0

        def store_out(row, part, value):
            stage[row - reach - group * GROUP, pl.ds(part, PART)] = value[:, :width]

        lax.fori_loop(begins[0], ends[0], average, 0)
        blur(est0, 0, r1, radius, begins[1], ends[1])
        adjoint(r1, radius, est0, 0, store_e1, begins[2], ends[2])
        blur(e1, 2 * radius, r2, 3 * radius, begins[3], ends[3])
        adjoint(r2, 3 * radius, e1, 2 * radius, store_out, begins[4], ends[4])
        for part in range(0, planes, GROUP):
            turned[group, pl.ds(part, GROUP)] = jnp.swapaxes(stage[:, pl.ds(part, GROUP)], 0, 1)
        place = out_ref.at[:, pl.ds(group * GROUP, GROUP), columns]
        keep = pltpu.make_async_copy(turned.at[group], place, own_sems.at[group])
        send = pltpu.make_async_remote_copy(
            src_ref=turned.at[group], dst_ref=place, send_sem=send_sems.at[group],
            recv_sem=recv_sems.at[group], device_id={"view": 1 - view_at},
            device_id_type=pl.DeviceIdType.MESH)
        send.start()
        keep.start()
        sends += [keep, send]
    for send in sends:
        send.wait()


def slab(n_z, radius, rows, taps, segments, strips):
    planes, width = segments[0].shape[1:]
    lanes = width + LANES
    reach = 4 * radius
    groups = rows // GROUP
    any_space = pl.BlockSpec(memory_space=pl.ANY)
    vmem = pl.BlockSpec(memory_space=pltpu.VMEM)
    in_specs = [pl.BlockSpec(memory_space=pltpu.SMEM)]
    in_specs += [any_space] * len(segments) + [vmem] * len(strips)
    n = [rows + 2 * k * radius for k in range(5)]
    return pl.pallas_call(
        functools.partial(slab_kernel, n_z, radius, rows),
        out_shape=jax.ShapeDtypeStruct((planes, rows, 2 * width), F32),
        in_specs=in_specs,
        out_specs=any_space,
        scratch_shapes=[
            pltpu.VMEM((2, n[4], planes, lanes), F32),
            pltpu.VMEM((n[4], planes, lanes), F32),
            pltpu.VMEM((2, n[3], planes, lanes), F32),
            pltpu.VMEM((n[2], planes, lanes), F32),
            pltpu.VMEM((2, n[1], planes, lanes), F32),
            pltpu.VMEM((GROUP, planes, width), F32),
            pltpu.VMEM((groups, planes, GROUP, width), F32),
            pltpu.VMEM((2, 2, planes, 3 * planes), BF16),
            pltpu.SemaphoreType.DMA((len(segments),)),
            pltpu.SemaphoreType.DMA((groups,)),
            pltpu.SemaphoreType.DMA((groups,)),
            pltpu.SemaphoreType.DMA((groups,)),
        ],
        cost_estimate=pl.CostEstimate(
            flops=sum(n[:4]) * 2 * planes * lanes * 6000,
            bytes_accessed=2 * n[4] * planes * lanes * 4, transcendentals=0),
        compiler_params=pltpu.CompilerParams(
            collective_id=0, has_side_effects=True, vmem_limit_bytes=50 * 2**20),
    )(taps, *segments, *strips)


def half_by_rows(recorded, which, begin, size):
    planes, _, cols = recorded.shape
    half = cols // 2

    def body(which_ref, in_ref, out_ref):
        out_ref[...] = jnp.swapaxes(in_ref[...], 0, 1)

    return pl.pallas_call(
        body,
        out_shape=jax.ShapeDtypeStruct((size, planes, half), F32),
        grid_spec=pltpu.PrefetchScalarGridSpec(
            num_scalar_prefetch=1,
            grid=(size // GROUP,),
            in_specs=[pl.BlockSpec(
                (planes, GROUP, half), lambda g, w: (0, begin // GROUP + g, w[0]))],
            out_specs=pl.BlockSpec((GROUP, planes, half), lambda g, w: (g, 0, 0)),
        ),
        cost_estimate=pl.CostEstimate(
            flops=0, bytes_accessed=size * planes * half * 8, transcendentals=0),
    )(which.reshape(1), recorded)


def packed_edges(low_rows, high_rows, reach):
    size, planes, half = low_rows.shape
    groups = size // GROUP

    def body(*refs):
        lane = lax.broadcasted_iota(jnp.int32, (GROUP, planes, LANES), 2)
        for side in range(2):
            keep = lane < reach if side == 0 else lane >= LANES - reach
            total = jnp.zeros((GROUP, planes, LANES), F32)
            for group in range(2 * groups):
                ref = refs[2 * side + group // groups]
                value = jnp.where(keep, ref[pl.ds(group % groups * GROUP, GROUP)], 0.0)
                if group:
                    value = pltpu.roll(value, LANES // PACK * group, 2)
                total = total + value
            refs[4 + side][...] = total

    first = pl.BlockSpec((size, planes, LANES), lambda g: (0, 0, 0))
    last = pl.BlockSpec((size, planes, LANES), lambda g: (0, 0, half // LANES - 1))
    edge = pl.BlockSpec((GROUP, planes, LANES), lambda g: (0, 0, 0))
    return pl.pallas_call(
        body,
        out_shape=[jax.ShapeDtypeStruct((GROUP, planes, LANES), F32)] * 2,
        grid=(1,),
        in_specs=[first, first, last, last],
        out_specs=[edge, edge],
    )(low_rows, high_rows, low_rows, high_rows)


def neighbours(low_edge, high_edge, axis):
    count = lax.axis_size(axis)
    forward = [(i, i + 1) for i in range(count - 1)]
    backward = [(i + 1, i) for i in range(count - 1)]
    return lax.ppermute(high_edge, axis, forward), lax.ppermute(low_edge, axis, backward)


def swap(value):
    return lax.ppermute(value, "view", [(0, 1), (1, 0)])


def per_device(views_data, psf_axial, psf_rows, psf_cols):
    recorded = views_data[0]
    planes, rows, cols = recorded.shape
    radius = psf_rows.shape[1] // 2
    reach = 4 * radius
    half = cols // 2
    mid = rows // 2
    mine = (lax.axis_index("view") + lax.axis_index("tx")) % 2

    sent_high = half_by_rows(recorded, 1 - mine, mid, mid)
    got_high = swap(sent_high)
    sent_low = half_by_rows(recorded, 1 - mine, 0, mid)
    got_low = swap(sent_low)
    own_high = half_by_rows(recorded, mine, mid, mid)
    own_low = half_by_rows(recorded, mine, 0, mid)

    own_taps = jnp.concatenate([
        psf_axial[0] / jnp.sum(psf_axial[0]), psf_rows[0] / jnp.sum(psf_rows[0]),
        psf_cols[0] / jnp.sum(psf_cols[0])])
    taps = jnp.stack([own_taps, swap(own_taps)])

    def extended(low, high):
        above, below = neighbours(low[:reach], high[mid - reach:], "ty")
        return above, low, high, below

    segments_own = extended(own_low, own_high)
    segments_got = extended(got_low, got_high)

    own_first, own_last = packed_edges(own_low, own_high, reach)
    sent_first, sent_last = packed_edges(sent_low, sent_high, reach)
    left = mine == 0
    before, after = neighbours(
        jnp.where(left, own_first, sent_first), jnp.where(left, sent_last, own_last), "tx")
    beside_left = before + jnp.where(left, sent_first, own_first)
    beside_right = jnp.where(left, own_last, sent_last) + after
    strip_own = jnp.where(left, beside_left, beside_right)
    strip_got = swap(jnp.where(left, beside_right, beside_left))
    strips = []
    for strip in (strip_own, strip_got):
        above, below = neighbours(strip, strip, "ty")
        strips += [above, strip, below]

    return slab(
        psf_axial.shape[1], radius, rows, taps, segments_own + segments_got, strips)


def solution(mesh):
    placed = (P("view", None, "ty", "tx"), P("view", None), P("view", None), P("view", None))
    return jax.shard_map(
        per_device, mesh=mesh, in_specs=placed, out_specs=P(None, "ty", "tx"), check_vma=False
    )
```

```python
import functools

import jax
import jax.numpy as jnp
from jax import lax
from jax.experimental import pallas as pl
from jax.experimental.pallas import tpu as pltpu
from jax.sharding import PartitionSpec as P

LANES = 128
GROUP = 8
ROWS = 4
PART = 16
PACK = 4
F32 = jnp.float32
BF16 = jnp.bfloat16


def split(value):
    high = value.astype(BF16)
    low = (value - high.astype(F32)).astype(BF16)
    return high, low


def axial_matrix(taps_ref, view, direction, planes, count):
    radius = count // 2
    i = lax.broadcasted_iota(jnp.int32, (planes, planes), 0)
    j = lax.broadcasted_iota(jnp.int32, (planes, planes), 1)
    offset = (j - i if direction == 0 else i - j) + radius
    matrix = jnp.zeros((planes, planes), F32)
    for tap in range(count):
        matrix = jnp.where(offset == tap, taps_ref[view, tap], matrix)
    high, low = split(matrix)
    return jnp.concatenate([high, high, low], axis=1)


def column_matrix(taps_ref, base, view, direction, lanes, count):
    radius = count // 2
    i = lax.broadcasted_iota(jnp.int32, (lanes, lanes), 0)
    j = lax.broadcasted_iota(jnp.int32, (lanes, lanes), 1)
    offset = (i - j if direction == 0 else j - i) + radius
    offset = jnp.where(offset < 0, offset + lanes, offset)
    offset = jnp.where(offset >= lanes, offset - lanes, offset)
    matrix = jnp.zeros((lanes, lanes), F32)
    for tap in range(count):
        matrix = jnp.where(offset == tap, taps_ref[view, base + tap], matrix)
    high, low = split(matrix)
    return jnp.concatenate([high, high, low], axis=0)


def slab_kernel(n_z, radius, rows, taps_ref, *refs):
    segments = (refs[0:4], refs[4:7])
    strips = (refs[7:10], refs[10:13])
    (out_ref, rec, est0, r1, e1, r2, stage, turned, wz, bx,
     in_sems, own_sems, send_sems, recv_sems, rows_sems) = refs[13:]
    reach = 4 * radius
    taps = 2 * radius + 1
    n_rec, planes, lanes = rec.shape[1:]
    width = lanes - LANES
    groups = rows // GROUP
    view_at = lax.axis_index("view")
    mine = (view_at + lax.axis_index("tx")) % 2
    columns = pl.ds(pl.multiple_of(mine * width, LANES), width)

    ty = lax.axis_index("ty")
    has_above = ty > 0
    has_below = ty < lax.axis_size("ty") - 1
    barrier = pltpu.get_barrier_semaphore()
    pl.semaphore_signal(
        barrier, inc=1, device_id={"view": 1 - view_at}, device_id_type=pl.DeviceIdType.MESH)
    for there, step in ((has_above, -1), (has_below, 1)):
        @pl.when(there)
        def _():
            pl.semaphore_signal(
                barrier, inc=1, device_id={"ty": ty + step},
                device_id_type=pl.DeviceIdType.MESH)
    inner = has_above & has_below

    @pl.when(inner)
    def _():
        pl.semaphore_wait(barrier, 3)

    @pl.when(jnp.logical_not(inner))
    def _():
        pl.semaphore_wait(barrier, 2)

    past = pl.ds(reach + rows, reach)
    rows_up = pltpu.make_async_remote_copy(
        src_ref=segments[1][1].at[pl.ds(0, reach)],
        dst_ref=rec.at[1, past, :, pl.ds(0, width)],
        send_sem=rows_sems.at[0], recv_sem=rows_sems.at[1],
        device_id={"ty": ty - 1}, device_id_type=pl.DeviceIdType.MESH)

    @pl.when(has_above)
    def _():
        rows_up.start()

    @pl.when(jnp.logical_not(has_below))
    def _():
        rec[1, past, :, :width] = jnp.zeros((reach, planes, width), F32)

    copies = []
    for view in range(2):
        begin = 0
        for segment in segments[view]:
            size = segment.shape[0]
            copies.append(pltpu.make_async_copy(
                segment, rec.at[view, pl.ds(begin, size), :, pl.ds(0, width)],
                in_sems.at[len(copies)]))
            begin += size
    for copy in copies:
        copy.start()

    for view in range(2):
        for direction in range(2):
            wz[view, direction] = axial_matrix(taps_ref, view, direction, planes, n_z)
    for direction in range(2):
        bx[direction] = column_matrix(taps_ref, n_z + taps, 0, direction, lanes, taps)

    lane = lax.broadcasted_iota(jnp.int32, (planes, LANES), 1)
    beside = (lane < reach) | (lane >= LANES - reach)
    for view in range(2):
        above, mid, below = strips[view]
        for at in range(n_rec):
            row = at - reach
            if row < 0:
                source, row = above, row + rows
            elif row >= rows:
                source, row = below, row - rows
            else:
                source = mid
            group, row = divmod(row, GROUP)
            value = source[row]
            if group:
                value = pltpu.roll(value, LANES - LANES // PACK * group, 1)
            rec[view, at, :, width:] = jnp.where(beside, value, 0.0)

    for copy in copies:
        copy.wait()

    def tap_of(base, view, direction, tap):
        return taps_ref[view, base + (tap if direction == 0 else taps - 1 - tap)]

    def rows_and_planes(load, view, direction):
        highs, lows = [], []
        for part in range(0, planes, PART):
            total = tap_of(n_z, view, direction, 0) * load(0, part)
            for tap in range(1, taps):
                total = total + tap_of(n_z, view, direction, tap) * load(tap, part)
            high, low = split(total)
            highs.append(high)
            lows.append(low)
        return jnp.dot(
            wz[view, direction], jnp.concatenate(highs + lows + highs, axis=0),
            preferred_element_type=F32)

    def by_matrix(fields, direction):
        parts = []
        for field in fields:
            high, low = split(field)
            parts.append(jnp.concatenate([high, low, high], axis=1))
        product = jnp.dot(
            jnp.concatenate(parts, axis=0), bx[direction], preferred_element_type=F32)
        return [product[k * planes:(k + 1) * planes] for k in range(len(fields))]

    def over_columns(field, view, direction):
        total = tap_of(n_z + taps, view, direction, radius) * field
        for tap in range(taps):
            if tap != radius:
                total = total + tap_of(n_z + taps, view, direction, tap) * pltpu.roll(
                    field, (radius - tap) % lanes, 1)
        return total

    def by_rows(begin, end, body):
        full = (end - begin) // ROWS

        def step(index, _):
            body([begin + index * ROWS + k for k in range(ROWS)])
            return 0

        lax.fori_loop(0, full, step, 0)
        if begin + full * ROWS < end:
            body(list(range(begin + full * ROWS, end)))

    def blur(source, source_at, target, target_at, begin, end):
        def body(at):
            passed = [[rows_and_planes(
                lambda j, part: source[row - radius - source_at + j, pl.ds(part, PART)], view, 0)
                for view in range(2)] for row in at]
            done = by_matrix([fields[0] for fields in passed], 0)
            for row, fields, first in zip(at, passed, done):
                for view in range(2):
                    for part in range(0, planes, PART):
                        if view == 0:
                            blurred = first[part:part + PART]
                        else:
                            blurred = over_columns(fields[1][part:part + PART], 1, 0)
                        recorded = rec[view, row, pl.ds(part, PART)]
                        inverse = pl.reciprocal(blurred, approx=True)
                        inverse = inverse * (2.0 - blurred * inverse)
                        target[view, row - target_at, pl.ds(part, PART)] = jnp.where(
                            recorded > 0, recorded * inverse, 0.0)
        by_rows(begin, end, body)

    def adjoint(source, source_at, estimate, estimate_at, store, begin, end):
        def body(at):
            passed = [[rows_and_planes(
                lambda j, part: source[
                    view, row - radius - source_at + j, pl.ds(part, PART)], view, 1)
                for view in range(2)] for row in at]
            done = by_matrix([fields[0] for fields in passed], 1)
            for row, fields, first in zip(at, passed, done):
                for part in range(0, planes, PART):
                    factor = (first[part:part + PART]
                              + over_columns(fields[1][part:part + PART], 1, 1))
                    old = estimate[row - estimate_at, pl.ds(part, PART)]
                    store(row, part, old * (factor * 0.5))
        by_rows(begin, end, body)

    def store_e1(row, part, value):
        e1[row - 2 * radius, pl.ds(part, PART)] = value

    sends = []
    for group in range(groups):
        ends = [(group + 1) * GROUP + reach + k * radius for k in (4, 3, 2, 1, 0)]
        begins = [0 if group == 0 else end - GROUP for end in ends]
        if group == 0:
            begins = [k * radius for k in range(5)]

        def average(row, _):
            est0[row] = (rec[0, row] + rec[1, row]) * 0.5
            return 0

        def store_out(row, part, value):
            stage[row - reach - group * GROUP, pl.ds(part, PART)] = value[:, :width]

        if begins[0] <= reach + rows < ends[0]:
            @pl.when(has_below)
            def _():
                rows_up.wait_recv()
        lax.fori_loop(begins[0], ends[0], average, 0)
        blur(est0, 0, r1, radius, begins[1], ends[1])
        adjoint(r1, radius, est0, 0, store_e1, begins[2], ends[2])
        blur(e1, 2 * radius, r2, 3 * radius, begins[3], ends[3])
        adjoint(r2, 3 * radius, e1, 2 * radius, store_out, begins[4], ends[4])
        for part in range(0, planes, GROUP):
            turned[group, pl.ds(part, GROUP)] = jnp.swapaxes(stage[:, pl.ds(part, GROUP)], 0, 1)
        place = out_ref.at[:, pl.ds(group * GROUP, GROUP), columns]
        keep = pltpu.make_async_copy(turned.at[group], place, own_sems.at[group])
        send = pltpu.make_async_remote_copy(
            src_ref=turned.at[group], dst_ref=place, send_sem=send_sems.at[group],
            recv_sem=recv_sems.at[group], device_id={"view": 1 - view_at},
            device_id_type=pl.DeviceIdType.MESH)
        send.start()
        keep.start()
        sends += [keep, send]
    for send in sends:
        send.wait()

    @pl.when(has_above)
    def _():
        rows_up.wait_send()


def slab(n_z, radius, rows, taps, segments, strips):
    planes, width = segments[0].shape[1:]
    lanes = width + LANES
    reach = 4 * radius
    groups = rows // GROUP
    any_space = pl.BlockSpec(memory_space=pl.ANY)
    vmem = pl.BlockSpec(memory_space=pltpu.VMEM)
    in_specs = [pl.BlockSpec(memory_space=pltpu.SMEM)]
    in_specs += [any_space] * len(segments) + [vmem] * len(strips)
    n = [rows + 2 * k * radius for k in range(5)]
    return pl.pallas_call(
        functools.partial(slab_kernel, n_z, radius, rows),
        out_shape=jax.ShapeDtypeStruct((planes, rows, 2 * width), F32),
        in_specs=in_specs,
        out_specs=any_space,
        scratch_shapes=[
            pltpu.VMEM((2, n[4], planes, lanes), F32),
            pltpu.VMEM((n[4], planes, lanes), F32),
            pltpu.VMEM((2, n[3], planes, lanes), F32),
            pltpu.VMEM((n[2], planes, lanes), F32),
            pltpu.VMEM((2, n[1], planes, lanes), F32),
            pltpu.VMEM((GROUP, planes, width), F32),
            pltpu.VMEM((groups, planes, GROUP, width), F32),
            pltpu.VMEM((2, 2, planes, 3 * planes), BF16),
            pltpu.VMEM((2, 3 * lanes, lanes), BF16),
            pltpu.SemaphoreType.DMA((len(segments),)),
            pltpu.SemaphoreType.DMA((groups,)),
            pltpu.SemaphoreType.DMA((groups,)),
            pltpu.SemaphoreType.DMA((groups,)),
            pltpu.SemaphoreType.DMA((2,)),
        ],
        cost_estimate=pl.CostEstimate(
            flops=sum(n[:4]) * 2 * planes * lanes * 6000,
            bytes_accessed=2 * n[4] * planes * lanes * 4, transcendentals=0),
        compiler_params=pltpu.CompilerParams(
            collective_id=0, has_side_effects=True, vmem_limit_bytes=54 * 2**20),
    )(taps, *segments, *strips)


def half_by_rows(recorded, which, begin, size):
    planes, _, cols = recorded.shape
    half = cols // 2

    def body(which_ref, in_ref, out_ref):
        out_ref[...] = jnp.swapaxes(in_ref[...], 0, 1)

    return pl.pallas_call(
        body,
        out_shape=jax.ShapeDtypeStruct((size, planes, half), F32),
        grid_spec=pltpu.PrefetchScalarGridSpec(
            num_scalar_prefetch=1,
            grid=(size // GROUP,),
            in_specs=[pl.BlockSpec(
                (planes, GROUP, half), lambda g, w: (0, begin // GROUP + g, w[0]))],
            out_specs=pl.BlockSpec((GROUP, planes, half), lambda g, w: (g, 0, 0)),
        ),
        cost_estimate=pl.CostEstimate(
            flops=0, bytes_accessed=size * planes * half * 8, transcendentals=0),
    )(which.reshape(1), recorded)


def packed_edges(low_rows, high_rows, reach):
    size, planes, half = low_rows.shape
    groups = size // GROUP

    def body(*refs):
        lane = lax.broadcasted_iota(jnp.int32, (GROUP, planes, LANES), 2)
        for side in range(2):
            keep = lane < reach if side == 0 else lane >= LANES - reach
            total = jnp.zeros((GROUP, planes, LANES), F32)
            for group in range(2 * groups):
                ref = refs[2 * side + group // groups]
                value = jnp.where(keep, ref[pl.ds(group % groups * GROUP, GROUP)], 0.0)
                if group:
                    value = pltpu.roll(value, LANES // PACK * group, 2)
                total = total + value
            refs[4 + side][...] = total

    first = pl.BlockSpec((size, planes, LANES), lambda g: (0, 0, 0))
    last = pl.BlockSpec((size, planes, LANES), lambda g: (0, 0, half // LANES - 1))
    edge = pl.BlockSpec((GROUP, planes, LANES), lambda g: (0, 0, 0))
    return pl.pallas_call(
        body,
        out_shape=[jax.ShapeDtypeStruct((GROUP, planes, LANES), F32)] * 2,
        grid=(1,),
        in_specs=[first, first, last, last],
        out_specs=[edge, edge],
    )(low_rows, high_rows, low_rows, high_rows)


def neighbours(low_edge, high_edge, axis):
    count = lax.axis_size(axis)
    forward = [(i, i + 1) for i in range(count - 1)]
    backward = [(i + 1, i) for i in range(count - 1)]
    return lax.ppermute(high_edge, axis, forward), lax.ppermute(low_edge, axis, backward)


def swap(value):
    return lax.ppermute(value, "view", [(0, 1), (1, 0)])


def per_device(views_data, psf_axial, psf_rows, psf_cols):
    recorded = views_data[0]
    planes, rows, cols = recorded.shape
    radius = psf_rows.shape[1] // 2
    reach = 4 * radius
    half = cols // 2
    mid = rows // 2
    mine = (lax.axis_index("view") + lax.axis_index("tx")) % 2

    sent_high = half_by_rows(recorded, 1 - mine, mid, mid)
    got_high = swap(sent_high)
    sent_low = half_by_rows(recorded, 1 - mine, 0, mid)
    got_low = swap(sent_low)
    own_high = half_by_rows(recorded, mine, mid, mid)
    own_low = half_by_rows(recorded, mine, 0, mid)

    own_taps = jnp.concatenate([
        psf_axial[0] / jnp.sum(psf_axial[0]), psf_rows[0] / jnp.sum(psf_rows[0]),
        psf_cols[0] / jnp.sum(psf_cols[0])])
    taps = jnp.stack([own_taps, swap(own_taps)])

    above, below = neighbours(own_low[:reach], own_high[mid - reach:], "ty")
    got_high, above, below = lax.optimization_barrier((got_high, above, below))
    segments = [above, own_low, own_high, below]
    above = lax.ppermute(
        got_high[mid - reach:], "ty", [(i, i + 1) for i in range(lax.axis_size("ty") - 1)])
    segments += [above, got_low, got_high]

    own_first, own_last = packed_edges(own_low, own_high, reach)
    sent_first, sent_last = packed_edges(sent_low, sent_high, reach)
    left = mine == 0
    before, after = neighbours(
        jnp.where(left, own_first, sent_first), jnp.where(left, sent_last, own_last), "tx")
    beside_left = before + jnp.where(left, sent_first, own_first)
    beside_right = jnp.where(left, own_last, sent_last) + after
    strip_own = jnp.where(left, beside_left, beside_right)
    strip_got = swap(jnp.where(left, beside_right, beside_left))
    strips = []
    for strip in (strip_own, strip_got):
        above, below = neighbours(strip, strip, "ty")
        strips += [above, strip, below]

    return slab(
        psf_axial.shape[1], radius, rows, taps, segments, strips)


def solution(mesh):
    placed = (P("view", None, "ty", "tx"), P("view", None), P("view", None), P("view", None))
    return jax.shard_map(
        per_device, mesh=mesh, in_specs=placed, out_specs=P(None, "ty", "tx"), check_vma=False
    )
```
